32 devices in a mesh: bx: 8 (over y, x, core), by: 4 (over z).
Axes of the slice: x: 2, y: 2, z: 4, core: 2. Of those that a mesh axis runs over, the one named last changes fastest.
Arguments:
- adjoint_start: float32 [6, 128, 64, 128], P(None, 'bx', 'by'), may hold values from -6 to 6
- objective_grad: float32 [6, 128, 64, 128], P(None, 'bx', 'by'), may hold values from -4 to 4
- spectral_radius: float32 [3, 128, 64, 128], P(None, 'bx', 'by'), may hold values from 0.5 to 4
- local_step: float32 [128, 64, 128], P('bx', 'by'), may hold values from 0.02 to 0.12
- flux_jacobian: float32 [3, 6, 6], replicated, may hold values from -2.5 to 2.5
- face_orient: int32 [8, 2], P('bx'), may hold values from 0 to 1, as said below
- wall_count: int32 [8, 4], P('bx', 'by'), may hold values from 0 to 256
- face_patch: int32 [128, 64], P('bx', 'by'), may hold values from 0 to 127
- face_area: float32 [128, 64], P('bx', 'by'), may hold values from 1 to 10
- force_weight: float32 [6], replicated, may hold values from -3 to 3
Outputs:
- adjoint_next: float32 [6, 128, 64, 128], P(None, 'bx', 'by')
- patch_force: float32 [128], P(('bx', 'by'))
The draws below stay inside these ranges and needn't reach their ends.
Inputs may be any that keep to these rules, and one draw needn't show every extreme that they name: face_orient[a, 1] equals face_orient[a + 1, 0]; a 1 marks a face between block rows whose matched cells run in reverse order along the third direction.
All inputs are finite; a program needn't handle non-finite values.
Results may differ from the reference program's by a relative error of at most 0.00012.
Values sent between devices are 32-bit elements; how exact they have to be, the bound alone decides.
A program may use at most 64 MiB of HBM per device.

```python
import math
import jax
import jax.numpy as jnp
from jax import lax

FIELDS = 6
CI = 16
CJ = 16
CK = 128
NX = 128
NY = 64
PATCHES = 128
N_BX = 8
N_BY = 4


def draw_face_orient(key, part):
    flags = jax.random.randint(key, (N_BX + 1,), 0, 2)
    return jnp.stack([flags[:-1], flags[1:]], axis=1).astype(jnp.int32)


def with_ends(drawn, own_key, low, largest):
    longest = drawn.shape.index(max(drawn.shape))
    spots = []
    for shift in (0, 1):
        where = [jax.random.randint(jax.random.fold_in(own_key, axis), (), 0, length) for axis, length in enumerate(drawn.shape)]
        where[longest] = (where[longest] + shift) % drawn.shape[longest]
        spots.append(tuple(where))
    return drawn.at[spots[0]].set(low).at[spots[1]].set(largest)


def levels(rng, extent, cuts, low, top_value):
    gain, own = 1.0, jax.random.fold_in(rng, 6)
    for axis_at, parts in cuts:
        steps = jnp.exp(jax.random.uniform(jax.random.fold_in(own, axis_at), (parts,), jnp.float32, low / len(cuts), top_value / len(cuts)))
        gain = gain * jnp.repeat(steps, extent[axis_at] // parts).reshape([-1 if axis == axis_at else 1 for axis in range(len(extent))])
    return gain


def normal_values(rng, dims, scale, limit, shards=(), dtype=jnp.bfloat16):
    drawn = jax.random.normal(rng, dims, jnp.float32) * scale
    if len(shards) > 0:
        drawn = levels(rng, dims, shards, -0.22, 0.18) * drawn
    return jnp.clip(drawn, min=-limit, max=limit).astype(dtype)


def setup_inputs(seed: int = 0) -> dict:
    seeds = jax.random.split(jax.random.key(seed), 11)
    return {
        "adjoint_start": normal_values(seeds[0], (FIELDS, NX, NY, CK), 1.0, 6.0, ((1, 8), (2, 4)), jnp.float32),
        "objective_grad": normal_values(seeds[1], (FIELDS, NX, NY, CK), 0.5, 4.0, ((1, 8), (2, 4)), jnp.float32),
        "spectral_radius": jnp.clip(jnp.exp(math.log(4.0) - 2.0794415 * jax.random.uniform(seeds[2], (3, NX, NY, CK), jnp.float32) ** levels(seeds[2], (3, NX, NY, CK), ((1, 8), (2, 4)), -0.2, 0.2)), 0.5, 4.0),
        "local_step": jnp.clip(jnp.exp(math.log(0.12) - 1.7917595 * jax.random.uniform(seeds[3], (NX, NY, CK), jnp.float32) ** levels(seeds[3], (NX, NY, CK), ((0, 8), (1, 4)), -0.2, 0.2)), 0.02, 0.12),
        "flux_jacobian": normal_values(seeds[4], (3, FIELDS, FIELDS), FIELDS ** -0.5, 2.5, (), jnp.float32),
        "face_orient": draw_face_orient(jax.random.fold_in(seeds[10], 71), 0),
        "wall_count": with_ends(jax.random.randint(seeds[6], (N_BX, N_BY), 0, CI * CJ + 1), jax.random.fold_in(seeds[6], 1), 0, CI * CJ).astype(jnp.int32),
        "face_patch": with_ends(jax.random.randint(seeds[7], (NX, NY), 0, PATCHES), jax.random.fold_in(seeds[7], 1), 0, PATCHES - 1).astype(jnp.int32),
        "face_area": jnp.clip(jnp.exp(math.log(10.0) - 2.3025851 * jax.random.uniform(seeds[8], (NX, NY), jnp.float32) ** levels(seeds[8], (NX, NY), ((0, 8), (1, 4)), -0.2, 0.2)), 1.0, 10.0),
        "force_weight": normal_values(seeds[9], (FIELDS,), 1.0, 3.0, (), jnp.float32),
    }


EPS = 0.1


def shift_zero(field, offset, axis):
    count = field.shape[axis]
    widths = [(0, 0)] * field.ndim
    widths[axis] = (2, 2)
    padded = jnp.pad(field, widths)
    return lax.slice_in_dim(padded, 2 + offset, 2 + offset + count, axis=axis)


def across_rows(field, offset, face_orient):
    shifted = shift_zero(field, offset, 1)
    rowpos = jnp.arange(NX) % CI
    block_row = jnp.arange(NX) // CI
    if offset < 0:
        cross = rowpos < -offset
        flagged = face_orient[block_row, 0] == 1
    else:
        cross = rowpos >= CI - offset
        flagged = face_orient[block_row, 1] == 1
    use = (cross & flagged)[None, :, None, None]
    return jnp.where(use, jnp.flip(shifted, 3), shifted)


def transpose_apply(matrix, field):
    return jnp.einsum('fg,fxyz->gxyz', matrix, field, precision=lax.Precision.HIGHEST)


def operate(field, radius, flux_jacobian, face_orient):
    summed = jnp.zeros_like(field)
    for direction in range(3):
        if direction == 0:
            front_one = across_rows(field, 1, face_orient)
            back_one = across_rows(field, -1, face_orient)
            front_two = across_rows(field, 2, face_orient)
            back_two = across_rows(field, -2, face_orient)
        else:
            front_one = shift_zero(field, 1, direction + 1)
            back_one = shift_zero(field, -1, direction + 1)
            front_two = shift_zero(field, 2, direction + 1)
            back_two = shift_zero(field, -2, direction + 1)
        if direction == 2:
            coupled = transpose_apply(flux_jacobian[direction], front_one + back_one)
        else:
            coupled = transpose_apply(flux_jacobian[direction], front_one - back_one)
        fourth = front_two - 4.0 * front_one + 6.0 * field - 4.0 * back_one + back_two
        summed = summed + radius[direction] * (0.5 * coupled + EPS * fourth)
    return summed


def reference(adjoint_start, objective_grad, spectral_radius, local_step, flux_jacobian, face_orient, wall_count, face_patch, face_area, force_weight):
    counts_full = jnp.repeat(jnp.repeat(wall_count, CI, axis=0), CJ, axis=1)
    position = (jnp.arange(NX) % CI)[:, None] * CJ + (jnp.arange(NY) % CJ)[None, :]
    live = (position < counts_full).astype(jnp.float32)
    wall_adjoint = jnp.einsum('f,fxy->xy', force_weight, adjoint_start[:, :, :, 0], precision=lax.Precision.HIGHEST)
    weighted_area = live * face_area
    wall_value = weighted_area * wall_adjoint
    patch_ids = face_patch.reshape(-1).astype(jnp.int32)
    patch_sum = jax.ops.segment_sum(wall_value.reshape(-1), patch_ids, num_segments=PATCHES)
    patch_area = jax.ops.segment_sum(weighted_area.reshape(-1), patch_ids, num_segments=PATCHES)
    patch_force = patch_sum / (1.0 + patch_area)
    face_force = weighted_area * patch_force[face_patch]
    source = objective_grad.at[:, :, :, 0].add(force_weight[:, None, None] * face_force[None])
    section_one = adjoint_start - 0.5 * local_step * (operate(adjoint_start, spectral_radius, flux_jacobian, face_orient) + source)
    adjoint_next = adjoint_start - local_step * (operate(section_one, spectral_radius, flux_jacobian, face_orient) + source)
    return adjoint_next, patch_force
```

```python
import functools

import jax
import jax.numpy as jnp
from jax import lax
from jax.experimental import pallas as pl
from jax.experimental.pallas import tpu as pltpu
from jax.sharding import PartitionSpec as P

P_DEV = 4
EPS = 0.1
FIELDS = 6
MESH = pl.DeviceIdType.MESH


def smooth_kernel(
    nx, ny, rows_i, rows_j,
    adj_hbm, obj_hbm, rad_hbm, step_hbm, patch_ref, area_ref, jac_ref, orient_ref, count_ref, weight_ref,
    out_ref, force_ref,
    adj, one, obj, rad, step, wall, pack1, pack2, halo1, halo2, turned, mine1, mine2, got1, got2,
    load_sem, hsend1, hrecv1, hsend2, hrecv2, psend1, precv1, psend2, precv2,
):
    cells = rows_i * rows_j
    pad = 2 * rows_j
    lanes = adj.shape[2]
    at_x = lax.axis_index("bx")
    at_y = lax.axis_index("by")
    patch_total = P_DEV * nx * ny
    groups = -(-patch_total // lanes)

    loads = [
        pltpu.make_async_copy(adj_hbm, adj.at[:, pl.ds(pad, cells), :], load_sem.at[0]),
        pltpu.make_async_copy(obj_hbm, obj, load_sem.at[1]),
        pltpu.make_async_copy(rad_hbm, rad, load_sem.at[2]),
        pltpu.make_async_copy(step_hbm, step, load_sem.at[3]),
    ]
    for copy in loads:
        copy.start()

    barrier = pltpu.get_barrier_semaphore()
    for o in range(1, nx):
        pl.semaphore_signal(barrier, inc=1, device_id=(lax.rem(at_x + o, nx), at_y), device_id_type=MESH)
    for o in range(1, ny):
        pl.semaphore_signal(barrier, inc=1, device_id=(at_x, lax.rem(at_y + o, ny)), device_id_type=MESH)

    zero = jnp.zeros((pad, lanes), jnp.float32)
    for ref in (adj, one):
        for f in range(FIELDS):
            ref[f, pl.ds(0, pad), :] = zero
            ref[f, pl.ds(pad + cells, pad), :] = zero
    pl.semaphore_wait(barrier, nx + ny - 2)

    has = [at_x > 0, at_x < nx - 1, at_y > 0, at_y < ny - 1]
    source_has = [has[1], has[0], has[3], has[2]]
    targets = [
        (lax.min(at_x + 1, nx - 1), at_y),
        (lax.max(at_x - 1, 0), at_y),
        (at_x, lax.min(at_y + 1, ny - 1)),
        (at_x, lax.max(at_y - 1, 0)),
    ]

    def halo_copies(low_rows, high_rows, pack, halo, send_sem, recv_sem):
        sources = [high_rows, low_rows, pack.at[1], pack.at[0]]
        return [
            pltpu.make_async_remote_copy(
                src_ref=sources[s], dst_ref=halo.at[s], send_sem=send_sem.at[s], recv_sem=recv_sem.at[s],
                device_id=targets[s], device_id_type=MESH,
            )
            for s in range(4)
        ]

    def start(copies, s):
        @pl.when(source_has[s])
        def _():
            copies[s].start()

    def pack_faces(ref, pack):
        for side, first in ((0, 0), (1, rows_j - 2)):
            for f in range(FIELDS):
                for layer in range(2):
                    pack[side, f, pl.ds(layer * rows_i, rows_i), :] = ref[
                        f, pl.ds(pad + first + layer, rows_i, stride=rows_j), :
                    ]

    first_copies = halo_copies(
        adj_hbm.at[:, pl.ds(0, pad), :], adj_hbm.at[:, pl.ds(cells - pad, pad), :], pack1, halo1, hsend1, hrecv1
    )
    start(first_copies, 0)
    start(first_copies, 1)
    loads[0].wait()
    pack_faces(adj, pack1)
    start(first_copies, 2)
    start(first_copies, 3)

    weights = [weight_ref[f] for f in range(FIELDS)]
    patch_t = jnp.transpose(patch_ref[...])
    area_t = jnp.transpose(area_ref[...])
    spot = lax.broadcasted_iota(jnp.int32, (rows_j, rows_i), 1) * rows_j + lax.broadcasted_iota(
        jnp.int32, (rows_j, rows_i), 0
    )
    area_t = jnp.where(spot < count_ref[0, 0], area_t, 0.0)
    lane = lax.broadcasted_iota(jnp.int32, (rows_j, lanes), 1)
    second = lax.broadcasted_iota(jnp.int32, (rows_j, lanes), 0)
    sums = [jnp.zeros((rows_j, lanes), jnp.float32) for _ in range(groups)]
    areas = [jnp.zeros((rows_j, lanes), jnp.float32) for _ in range(groups)]
    for i in range(rows_i):
        weighted = weights[0] * adj[0, pl.ds(pad + i * rows_j, rows_j), :]
        for f in range(1, FIELDS):
            weighted = weighted + weights[f] * adj[f, pl.ds(pad + i * rows_j, rows_j), :]
        area = area_t[:, i : i + 1]
        value = area * weighted[:, 0:1]
        patch = patch_t[:, i : i + 1]
        for r in range(groups):
            hit = patch == lane + r * lanes
            sums[r] = sums[r] + jnp.where(hit, value, 0.0)
            areas[r] = areas[r] + jnp.where(hit, area, 0.0)
    for r in range(groups):
        mine1[pl.ds(r, 1), :] = jnp.sum(sums[r], axis=0, keepdims=True)
        mine1[pl.ds(groups + r, 1), :] = jnp.sum(areas[r], axis=0, keepdims=True)

    x_copies = [
        pltpu.make_async_remote_copy(
            src_ref=mine1, dst_ref=got1.at[o - 1], send_sem=psend1.at[o - 1], recv_sem=precv1.at[o - 1],
            device_id=(lax.rem(at_x + o, nx), at_y), device_id_type=MESH,
        )
        for o in range(1, nx)
    ]
    y_copies = [
        pltpu.make_async_remote_copy(
            src_ref=mine2, dst_ref=got2.at[o - 1], send_sem=psend2.at[o - 1], recv_sem=precv2.at[o - 1],
            device_id=(at_x, lax.rem(at_y + o, ny)), device_id_type=MESH,
        )
        for o in range(1, ny)
    ]
    for copy in x_copies:
        copy.start()

    scale = 0.5 / EPS

    def coupled(direction, g, fields):
        total = (jac_ref[direction, 0, g] * scale) * fields[0]
        for f in range(1, FIELDS):
            total = total + (jac_ref[direction, f, g] * scale) * fields[f]
        return total

    def section(ref, target, offset, factor, with_wall, first_i, last_i):
        def body(i, carry):
            base = pl.multiple_of(i * rows_j, rows_j)

            def rows(f, shift):
                return ref[f, pl.ds(base + (pad + shift), rows_j), :]

            center = [rows(f, 0) for f in range(FIELDS)]
            six = [6.0 * c for c in center]
            total = [None] * FIELDS
            for direction in range(3):
                near, far = [], []
                for f in range(FIELDS):
                    if direction == 0:
                        f1, b1, f2, b2 = (rows(f, s * rows_j) for s in (1, -1, 2, -2))
                    elif direction == 1:
                        f1 = jnp.where(second < rows_j - 1, rows(f, 1), 0.0)
                        b1 = jnp.where(second >= 1, rows(f, -1), 0.0)
                        f2 = jnp.where(second < rows_j - 2, rows(f, 2), 0.0)
                        b2 = jnp.where(second >= 2, rows(f, -2), 0.0)
                    else:
                        c = center[f]
                        f1 = jnp.where(lane < lanes - 1, pltpu.roll(c, lanes - 1, 1), 0.0)
                        b1 = jnp.where(lane >= 1, pltpu.roll(c, 1, 1), 0.0)
                        f2 = jnp.where(lane < lanes - 2, pltpu.roll(c, lanes - 2, 1), 0.0)
                        b2 = jnp.where(lane >= 2, pltpu.roll(c, 2, 1), 0.0)
                    both = f1 + b1
                    near.append(both if direction == 2 else f1 - b1)
                    far.append((f2 + b2) - 4.0 * both + six[f])
                radius = EPS * rad[direction, pl.ds(base, rows_j), :]
                for g in range(FIELDS):
                    term = radius * (far[g] + coupled(direction, g, near))
                    total[g] = term if direction == 0 else total[g] + term
            size = step[pl.ds(base, rows_j), :]
            if factor != 1.0:
                size = factor * size
            at_wall = wall[pl.ds(base, rows_j), :] if with_wall else None
            for g in range(FIELDS):
                whole = total[g] + obj[g, pl.ds(base, rows_j), :]
                if with_wall:
                    whole = whole + weights[g] * at_wall
                start_value = center[g] if ref is adj else adj[g, pl.ds(base + pad, rows_j), :]
                target[g, pl.ds(base + offset, rows_j), :] = start_value - size * whole
            return carry

        lax.fori_loop(first_i, last_i, body, 0)

    def turn(halo, side, flag):
        row = lax.broadcasted_iota(jnp.int32, (lanes, lanes), 0)
        col = lax.broadcasted_iota(jnp.int32, (lanes, lanes), 1)
        goal = jnp.where(flag == 1, lanes - 1 - col, col)
        matrix = jnp.where(row == goal, 1.0, 0.0).astype(jnp.float32)
        values = halo[side].reshape(FIELDS * pad, lanes)
        moved = jnp.dot(values, matrix, precision=lax.Precision.HIGHEST, preferred_element_type=jnp.float32)
        turned[...] = moved.reshape(FIELDS, pad, lanes)

    def correct(halo, side, target, offset, factor):
        direction, high = side // 2, side % 2
        count = rows_j if direction == 0 else rows_i
        layers = rows_i if direction == 0 else rows_j
        near_at, far_at = (0, count) if high else (count, 0)
        edge, inner = (layers - 1, layers - 2) if high else (0, 1)

        def at(layer, extra):
            if direction == 0:
                return pl.ds(extra + layer * rows_j, rows_j)
            return pl.ds(extra + layer, rows_i, stride=rows_j)

        def load(f, first):
            if direction == 0:
                return turned[f, pl.ds(first, count), :]
            return halo[side, f, pl.ds(first, count), :]

        near = [load(f, near_at) for f in range(FIELDS)]
        size_edge = (factor * EPS) * step[at(edge, 0), :] * rad[direction, at(edge, 0), :]
        size_inner = (factor * EPS) * step[at(inner, 0), :] * rad[direction, at(inner, 0), :]
        for g in range(FIELDS):
            mixed = coupled(direction, g, near)
            if not high:
                mixed = -mixed
            change = mixed + (load(g, far_at) - 4.0 * near[g])
            target[g, at(edge, offset), :] = target[g, at(edge, offset), :] - size_edge * change
            target[g, at(inner, offset), :] = target[g, at(inner, offset), :] - size_inner * near[g]

    def finish_halo(copies, halo, target, offset, factor):
        for s in range(4):
            @pl.when(has[s])
            def _(s=s):
                copies[s].wait_recv()
                if s < 2:
                    turn(halo, s, orient_ref[0, s])
                correct(halo, s, target, offset, factor)

    for copy in loads[1:]:
        copy.wait()
    half = rows_i // 2
    section(adj, one, pad, 0.5, False, 0, half)
    for copy in x_copies:
        copy.wait_recv()
    mine2[...] = functools.reduce(lambda a, b: a + b, [got1[o] for o in range(nx - 1)], mine1[...])
    for copy in y_copies:
        copy.start()
    section(adj, one, pad, 0.5, False, half, rows_i)
    finish_halo(first_copies, halo1, one, pad, 0.5)
    for copy in y_copies:
        copy.wait_recv()
    summed = functools.reduce(lambda a, b: a + b, [got2[o] for o in range(ny - 1)], mine2[...])
    force = summed[:groups] / (1.0 + summed[groups:])

    for i in range(rows_i):
        patch = patch_t[:, i : i + 1]
        hits = jnp.where(patch == lane, force[0:1], 0.0)
        for r in range(1, groups):
            hits = hits + jnp.where(patch == lane + r * lanes, force[r : r + 1], 0.0)
        face = area_t[:, i : i + 1] * jnp.sum(hits, axis=1, keepdims=True)
        face = jnp.where(lane == 0, face, 0.0)
        wall[pl.ds(i * rows_j, rows_j), :] = face
        moved = 0.5 * step[pl.ds(i * rows_j, rows_j), :] * face
        for f in range(FIELDS):
            at = pl.ds(pad + i * rows_j, rows_j)
            one[f, at, :] = one[f, at, :] - weights[f] * moved

    second_copies = halo_copies(
        one.at[:, pl.ds(pad, pad), :], one.at[:, pl.ds(cells, pad), :], pack2, halo2, hsend2, hrecv2
    )
    start(second_copies, 0)
    start(second_copies, 1)
    pack_faces(one, pack2)
    start(second_copies, 2)
    start(second_copies, 3)

    own = (at_x * ny + at_y) * P_DEV
    place = lax.broadcasted_iota(jnp.int32, (groups, lanes), 0) * lanes + lax.broadcasted_iota(
        jnp.int32, (groups, lanes), 1
    )
    for q in range(P_DEV):
        force_ref[q] = jnp.sum(jnp.where(place == own + q, force, 0.0))

    section(one, out_ref, 0, 1.0, True, 0, rows_i)
    finish_halo(second_copies, halo2, out_ref, 0, 1.0)

    for copies in (first_copies, second_copies):
        for s in range(4):
            @pl.when(source_has[s])
            def _(s=s, copies=copies):
                copies[s].wait_send()
    for copy in x_copies + y_copies:
        copy.wait_send()


def local(
    adjoint_start,
    objective_grad,
    spectral_radius,
    local_step,
    flux_jacobian,
    face_orient,
    wall_count,
    face_patch,
    face_area,
    force_weight,
):
    fields, rows_i, rows_j, lanes = adjoint_start.shape
    cells, pad = rows_i * rows_j, 2 * rows_j
    nx, ny = lax.axis_size("bx"), lax.axis_size("by")
    groups = -(-P_DEV * nx * ny // lanes)
    f32 = jnp.float32
    vmem = pl.BlockSpec(memory_space=pltpu.VMEM)
    smem = pl.BlockSpec(memory_space=pltpu.SMEM)
    anywhere = pl.BlockSpec(memory_space=pl.ANY)
    dma = pltpu.SemaphoreType.DMA
    result, force = pl.pallas_call(
        functools.partial(smooth_kernel, nx, ny, rows_i, rows_j),
        out_shape=(
            jax.ShapeDtypeStruct((fields, cells, lanes), f32),
            jax.ShapeDtypeStruct((P_DEV,), f32),
        ),
        in_specs=[anywhere] * 4 + [vmem] * 2 + [smem] * 4,
        out_specs=(vmem, smem),
        scratch_shapes=[
            pltpu.VMEM((fields, cells + 2 * pad, lanes), f32),
            pltpu.VMEM((fields, cells + 2 * pad, lanes), f32),
            pltpu.VMEM((fields, cells, lanes), f32),
            pltpu.VMEM((3, cells, lanes), f32),
            pltpu.VMEM((cells, lanes), f32),
            pltpu.VMEM((cells, lanes), f32),
            pltpu.VMEM((2, fields, 2 * rows_i, lanes), f32),
            pltpu.VMEM((2, fields, 2 * rows_i, lanes), f32),
            pltpu.VMEM((4, fields, pad, lanes), f32),
            pltpu.VMEM((4, fields, pad, lanes), f32),
            pltpu.VMEM((fields, pad, lanes), f32),
            pltpu.VMEM((2 * groups, lanes), f32),
            pltpu.VMEM((2 * groups, lanes), f32),
            pltpu.VMEM((nx - 1, 2 * groups, lanes), f32),
            pltpu.VMEM((ny - 1, 2 * groups, lanes), f32),
            dma((4,)), dma((4,)), dma((4,)), dma((4,)), dma((4,)),
            dma((nx - 1,)), dma((nx - 1,)), dma((ny - 1,)), dma((ny - 1,)),
        ],
        compiler_params=pltpu.CompilerParams(
            collective_id=0, has_side_effects=True, vmem_limit_bytes=32 * 1024 * 1024
        ),
    )(
        adjoint_start.reshape(fields, cells, lanes),
        objective_grad.reshape(fields, cells, lanes),
        spectral_radius.reshape(3, cells, lanes),
        local_step.reshape(cells, lanes),
        face_patch,
        face_area,
        flux_jacobian,
        face_orient,
        wall_count,
        force_weight,
    )
    return result.reshape(adjoint_start.shape), force


def solution(mesh):
    in_specs = (
        P(None, "bx", "by", None),
        P(None, "bx", "by", None),
        P(None, "bx", "by", None),
        P("bx", "by", None),
        P(),
        P("bx", None),
        P("bx", "by"),
        P("bx", "by"),
        P("bx", "by"),
        P(),
    )
    out_specs = (P(None, "bx", "by", None), P(("bx", "by")))
    return jax.shard_map(local, mesh=mesh, in_specs=in_specs, out_specs=out_specs, check_vma=False)
```

```python
import functools

import jax
import jax.numpy as jnp
from jax import lax
from jax.experimental import pallas as pl
from jax.experimental.pallas import tpu as pltpu
from jax.sharding import PartitionSpec as P

P_DEV = 4
EPS = 0.1
FIELDS = 6
MESH = pl.DeviceIdType.MESH


def smooth_kernel(
    nx, ny, rows_i, rows_j,
    adj_hbm, obj_hbm, rad_hbm, step_hbm, patch_hbm, area_hbm, jac_hbm, orient_hbm, count_hbm, weight_hbm,
    out_ref, force_ref,
    patch_ref, area_ref, jac_ref, orient_ref, count_ref, weight_ref,
    adj, one, obj, rad, step, wall, pack1, pack2, halo1, halo2, turned, mine1, mine2, got1, got2,
    load_sem, hsend1, hrecv1, hsend2, hrecv2, psend1, precv1, psend2, precv2,
):
    cells = rows_i * rows_j
    pad = 2 * rows_j
    lanes = adj.shape[2]
    at_x = lax.axis_index("bx")
    at_y = lax.axis_index("by")
    patch_total = P_DEV * nx * ny
    groups = -(-patch_total // lanes)

    small = [
        pltpu.make_async_copy(src, dst, load_sem.at[4 + n])
        for n, (src, dst) in enumerate((
            (weight_hbm, weight_ref), (count_hbm, count_ref), (patch_hbm, patch_ref), (area_hbm, area_ref),
            (jac_hbm, jac_ref), (orient_hbm, orient_ref),
        ))
    ]
    loads = [
        pltpu.make_async_copy(adj_hbm, adj.at[:, pl.ds(pad, cells), :], load_sem.at[0]),
        pltpu.make_async_copy(obj_hbm, obj, load_sem.at[1]),
        pltpu.make_async_copy(rad_hbm, rad, load_sem.at[2]),
        pltpu.make_async_copy(step_hbm, step, load_sem.at[3]),
    ]
    loads[0].start()
    for copy in small:
        copy.start()
    for copy in loads[1:]:
        copy.start()

    barrier = pltpu.get_barrier_semaphore()
    for o in range(1, nx):
        pl.semaphore_signal(barrier, inc=1, device_id=(lax.rem(at_x + o, nx), at_y), device_id_type=MESH)
    for o in range(1, ny):
        pl.semaphore_signal(barrier, inc=1, device_id=(at_x, lax.rem(at_y + o, ny)), device_id_type=MESH)

    zero = jnp.zeros((pad, lanes), jnp.float32)
    for ref in (adj, one):
        for f in range(FIELDS):
            ref[f, pl.ds(0, pad), :] = zero
            ref[f, pl.ds(pad + cells, pad), :] = zero
    pl.semaphore_wait(barrier, nx + ny - 2)

    has = [at_x > 0, at_x < nx - 1, at_y > 0, at_y < ny - 1]
    source_has = [has[1], has[0], has[3], has[2]]
    targets = [
        (lax.min(at_x + 1, nx - 1), at_y),
        (lax.max(at_x - 1, 0), at_y),
        (at_x, lax.min(at_y + 1, ny - 1)),
        (at_x, lax.max(at_y - 1, 0)),
    ]

    def halo_copies(low_rows, high_rows, pack, halo, send_sem, recv_sem):
        sources = [high_rows, low_rows, pack.at[1], pack.at[0]]
        return [
            pltpu.make_async_remote_copy(
                src_ref=sources[s], dst_ref=halo.at[s], send_sem=send_sem.at[s], recv_sem=recv_sem.at[s],
                device_id=targets[s], device_id_type=MESH,
            )
            for s in range(4)
        ]

    def start(copies, s):
        @pl.when(source_has[s])
        def _():
            copies[s].start()

    def pack_faces(ref, pack):
        for side, first in ((0, 0), (1, rows_j - 2)):
            for f in range(FIELDS):
                for layer in range(2):
                    pack[side, f, pl.ds(layer * rows_i, rows_i), :] = ref[
                        f, pl.ds(pad + first + layer, rows_i, stride=rows_j), :
                    ]

    first_copies = halo_copies(
        adj_hbm.at[:, pl.ds(0, pad), :], adj_hbm.at[:, pl.ds(cells - pad, pad), :], pack1, halo1, hsend1, hrecv1
    )
    start(first_copies, 0)
    start(first_copies, 1)
    loads[0].wait()
    pack_faces(adj, pack1)
    start(first_copies, 2)
    start(first_copies, 3)

    for copy in small:
        copy.wait()
    weights = [weight_ref[f] for f in range(FIELDS)]
    patch_t = jnp.transpose(patch_ref[...])
    area_t = jnp.transpose(area_ref[...])
    spot = lax.broadcasted_iota(jnp.int32, (rows_j, rows_i), 1) * rows_j + lax.broadcasted_iota(
        jnp.int32, (rows_j, rows_i), 0
    )
    area_t = jnp.where(spot < count_ref[0, 0], area_t, 0.0)
    lane = lax.broadcasted_iota(jnp.int32, (rows_j, lanes), 1)
    second = lax.broadcasted_iota(jnp.int32, (rows_j, lanes), 0)
    sums = [jnp.zeros((rows_j, lanes), jnp.float32) for _ in range(groups)]
    areas = [jnp.zeros((rows_j, lanes), jnp.float32) for _ in range(groups)]
    for i in range(rows_i):
        weighted = weights[0] * adj[0, pl.ds(pad + i * rows_j, rows_j), :]
        for f in range(1, FIELDS):
            weighted = weighted + weights[f] * adj[f, pl.ds(pad + i * rows_j, rows_j), :]
        area = area_t[:, i : i + 1]
        value = area * weighted[:, 0:1]
        patch = patch_t[:, i : i + 1]
        for r in range(groups):
            hit = patch == lane + r * lanes
            sums[r] = sums[r] + jnp.where(hit, value, 0.0)
            areas[r] = areas[r] + jnp.where(hit, area, 0.0)
    for r in range(groups):
        mine1[pl.ds(r, 1), :] = jnp.sum(sums[r], axis=0, keepdims=True)
        mine1[pl.ds(groups + r, 1), :] = jnp.sum(areas[r], axis=0, keepdims=True)

    x_copies = [
        pltpu.make_async_remote_copy(
            src_ref=mine1, dst_ref=got1.at[o - 1], send_sem=psend1.at[o - 1], recv_sem=precv1.at[o - 1],
            device_id=(lax.rem(at_x + o, nx), at_y), device_id_type=MESH,
        )
        for o in range(1, nx)
    ]
    y_copies = [
        pltpu.make_async_remote_copy(
            src_ref=mine2, dst_ref=got2.at[o - 1], send_sem=psend2.at[o - 1], recv_sem=precv2.at[o - 1],
            device_id=(at_x, lax.rem(at_y + o, ny)), device_id_type=MESH,
        )
        for o in range(1, ny)
    ]
    for copy in x_copies:
        copy.start()

    scale = 0.5 / EPS

    def coupled(direction, g, fields):
        total = (jac_ref[direction, 0, g] * scale) * fields[0]
        for f in range(1, FIELDS):
            total = total + (jac_ref[direction, f, g] * scale) * fields[f]
        return total

    def section(ref, target, offset, factor, with_wall, first_i, last_i):
        def body(i, carry):
            base = pl.multiple_of(i * rows_j, rows_j)

            def rows(f, shift):
                return ref[f, pl.ds(base + (pad + shift), rows_j), :]

            center = [rows(f, 0) for f in range(FIELDS)]
            six = [6.0 * c for c in center]
            total = [None] * FIELDS
            for direction in range(3):
                near, far = [], []
                for f in range(FIELDS):
                    if direction == 0:
                        f1, b1, f2, b2 = (rows(f, s * rows_j) for s in (1, -1, 2, -2))
                    elif direction == 1:
                        f1 = jnp.where(second < rows_j - 1, rows(f, 1), 0.0)
                        b1 = jnp.where(second >= 1, rows(f, -1), 0.0)
                        f2 = jnp.where(second < rows_j - 2, rows(f, 2), 0.0)
                        b2 = jnp.where(second >= 2, rows(f, -2), 0.0)
                    else:
                        c = center[f]
                        f1 = jnp.where(lane < lanes - 1, pltpu.roll(c, lanes - 1, 1), 0.0)
                        b1 = jnp.where(lane >= 1, pltpu.roll(c, 1, 1), 0.0)
                        f2 = jnp.where(lane < lanes - 2, pltpu.roll(c, lanes - 2, 1), 0.0)
                        b2 = jnp.where(lane >= 2, pltpu.roll(c, 2, 1), 0.0)
                    both = f1 + b1
                    near.append(both if direction == 2 else f1 - b1)
                    far.append((f2 + b2) - 4.0 * both + six[f])
                radius = EPS * rad[direction, pl.ds(base, rows_j), :]
                for g in range(FIELDS):
                    term = radius * (far[g] + coupled(direction, g, near))
                    total[g] = term if direction == 0 else total[g] + term
            size = step[pl.ds(base, rows_j), :]
            if factor != 1.0:
                size = factor * size
            at_wall = wall[pl.ds(base, rows_j), :] if with_wall else None
            for g in range(FIELDS):
                whole = total[g] + obj[g, pl.ds(base, rows_j), :]
                if with_wall:
                    whole = whole + weights[g] * at_wall
                start_value = center[g] if ref is adj else adj[g, pl.ds(base + pad, rows_j), :]
                target[g, pl.ds(base + offset, rows_j), :] = start_value - size * whole
            return carry

        lax.fori_loop(first_i, last_i, body, 0)

    def turn(halo, side, flag):
        row = lax.broadcasted_iota(jnp.int32, (lanes, lanes), 0)
        col = lax.broadcasted_iota(jnp.int32, (lanes, lanes), 1)
        goal = jnp.where(flag == 1, lanes - 1 - col, col)
        matrix = jnp.where(row == goal, 1.0, 0.0).astype(jnp.float32)
        values = halo[side].reshape(FIELDS * pad, lanes)
        moved = jnp.dot(values, matrix, precision=lax.Precision.HIGHEST, preferred_element_type=jnp.float32)
        turned[...] = moved.reshape(FIELDS, pad, lanes)

    def correct(halo, side, target, offset, factor):
        direction, high = side // 2, side % 2
        count = rows_j if direction == 0 else rows_i
        layers = rows_i if direction == 0 else rows_j
        near_at, far_at = (0, count) if high else (count, 0)
        edge, inner = (layers - 1, layers - 2) if high else (0, 1)

        def at(layer, extra):
            if direction == 0:
                return pl.ds(extra + layer * rows_j, rows_j)
            return pl.ds(extra + layer, rows_i, stride=rows_j)

        def load(f, first):
            if direction == 0:
                return turned[f, pl.ds(first, count), :]
            return halo[side, f, pl.ds(first, count), :]

        near = [load(f, near_at) for f in range(FIELDS)]
        size_edge = (factor * EPS) * step[at(edge, 0), :] * rad[direction, at(edge, 0), :]
        size_inner = (factor * EPS) * step[at(inner, 0), :] * rad[direction, at(inner, 0), :]
        for g in range(FIELDS):
            mixed = coupled(direction, g, near)
            if not high:
                mixed = -mixed
            change = mixed + (load(g, far_at) - 4.0 * near[g])
            target[g, at(edge, offset), :] = target[g, at(edge, offset), :] - size_edge * change
            target[g, at(inner, offset), :] = target[g, at(inner, offset), :] - size_inner * near[g]

    def finish_halo(copies, halo, target, offset, factor):
        for s in range(4):
            @pl.when(has[s])
            def _(s=s):
                copies[s].wait_recv()
                if s < 2:
                    turn(halo, s, orient_ref[0, s])
                correct(halo, s, target, offset, factor)

    for copy in loads[1:]:
        copy.wait()
    half = rows_i // 2
    section(adj, one, pad, 0.5, False, 0, half)
    for copy in x_copies:
        copy.wait_recv()
    mine2[...] = functools.reduce(lambda a, b: a + b, [got1[o] for o in range(nx - 1)], mine1[...])
    for copy in y_copies:
        copy.start()
    section(adj, one, pad, 0.5, False, half, rows_i)
    finish_halo(first_copies, halo1, one, pad, 0.5)
    for copy in y_copies:
        copy.wait_recv()
    summed = functools.reduce(lambda a, b: a + b, [got2[o] for o in range(ny - 1)], mine2[...])
    force = summed[:groups] / (1.0 + summed[groups:])

    for i in range(rows_i):
        patch = patch_t[:, i : i + 1]
        hits = jnp.where(patch == lane, force[0:1], 0.0)
        for r in range(1, groups):
            hits = hits + jnp.where(patch == lane + r * lanes, force[r : r + 1], 0.0)
        face = area_t[:, i : i + 1] * jnp.sum(hits, axis=1, keepdims=True)
        face = jnp.where(lane == 0, face, 0.0)
        wall[pl.ds(i * rows_j, rows_j), :] = face
        moved = 0.5 * step[pl.ds(i * rows_j, rows_j), :] * face
        for f in range(FIELDS):
            at = pl.ds(pad + i * rows_j, rows_j)
            one[f, at, :] = one[f, at, :] - weights[f] * moved

    second_copies = halo_copies(
        one.at[:, pl.ds(pad, pad), :], one.at[:, pl.ds(cells, pad), :], pack2, halo2, hsend2, hrecv2
    )
    start(second_copies, 0)
    start(second_copies, 1)
    pack_faces(one, pack2)
    start(second_copies, 2)
    start(second_copies, 3)

    own = (at_x * ny + at_y) * P_DEV
    place = lax.broadcasted_iota(jnp.int32, (groups, lanes), 0) * lanes + lax.broadcasted_iota(
        jnp.int32, (groups, lanes), 1
    )
    for q in range(P_DEV):
        force_ref[q] = jnp.sum(jnp.where(place == own + q, force, 0.0))

    section(one, out_ref, 0, 1.0, True, 0, rows_i)
    finish_halo(second_copies, halo2, out_ref, 0, 1.0)

    for copies in (first_copies, second_copies):
        for s in range(4):
            @pl.when(source_has[s])
            def _(s=s, copies=copies):
                copies[s].wait_send()
    for copy in x_copies + y_copies:
        copy.wait_send()


def local(
    adjoint_start,
    objective_grad,
    spectral_radius,
    local_step,
    flux_jacobian,
    face_orient,
    wall_count,
    face_patch,
    face_area,
    force_weight,
):
    fields, rows_i, rows_j, lanes = adjoint_start.shape
    cells, pad = rows_i * rows_j, 2 * rows_j
    nx, ny = lax.axis_size("bx"), lax.axis_size("by")
    groups = -(-P_DEV * nx * ny // lanes)
    f32 = jnp.float32
    vmem = pl.BlockSpec(memory_space=pltpu.VMEM)
    smem = pl.BlockSpec(memory_space=pltpu.SMEM)
    hbm = pl.BlockSpec(memory_space=pltpu.HBM)
    dma = pltpu.SemaphoreType.DMA
    result, force = pl.pallas_call(
        functools.partial(smooth_kernel, nx, ny, rows_i, rows_j),
        out_shape=(
            jax.ShapeDtypeStruct((fields, cells, lanes), f32),
            jax.ShapeDtypeStruct((P_DEV,), f32),
        ),
        in_specs=[hbm] * 10,
        out_specs=(vmem, smem),
        scratch_shapes=[
            pltpu.VMEM(face_patch.shape, jnp.int32),
            pltpu.VMEM(face_area.shape, f32),
            pltpu.SMEM(flux_jacobian.shape, f32),
            pltpu.SMEM(face_orient.shape, jnp.int32),
            pltpu.SMEM(wall_count.shape, jnp.int32),
            pltpu.SMEM(force_weight.shape, f32),
            pltpu.VMEM((fields, cells + 2 * pad, lanes), f32),
            pltpu.VMEM((fields, cells + 2 * pad, lanes), f32),
            pltpu.VMEM((fields, cells, lanes), f32),
            pltpu.VMEM((3, cells, lanes), f32),
            pltpu.VMEM((cells, lanes), f32),
            pltpu.VMEM((cells, lanes), f32),
            pltpu.VMEM((2, fields, 2 * rows_i, lanes), f32),
            pltpu.VMEM((2, fields, 2 * rows_i, lanes), f32),
            pltpu.VMEM((4, fields, pad, lanes), f32),
            pltpu.VMEM((4, fields, pad, lanes), f32),
            pltpu.VMEM((fields, pad, lanes), f32),
            pltpu.VMEM((2 * groups, lanes), f32),
            pltpu.VMEM((2 * groups, lanes), f32),
            pltpu.VMEM((nx - 1, 2 * groups, lanes), f32),
            pltpu.VMEM((ny - 1, 2 * groups, lanes), f32),
            dma((10,)), dma((4,)), dma((4,)), dma((4,)), dma((4,)),
            dma((nx - 1,)), dma((nx - 1,)), dma((ny - 1,)), dma((ny - 1,)),
        ],
        compiler_params=pltpu.CompilerParams(
            collective_id=0, has_side_effects=True, vmem_limit_bytes=62 * 1024 * 1024
        ),
    )(
        adjoint_start.reshape(fields, cells, lanes),
        objective_grad.reshape(fields, cells, lanes),
        spectral_radius.reshape(3, cells, lanes),
        local_step.reshape(cells, lanes),
        face_patch,
        face_area,
        flux_jacobian,
        face_orient,
        wall_count,
        force_weight,
    )
    return result.reshape(adjoint_start.shape), force


def solution(mesh):
    in_specs = (
        P(None, "bx", "by", None),
        P(None, "bx", "by", None),
        P(None, "bx", "by", None),
        P("bx", "by", None),
        P(),
        P("bx", None),
        P("bx", "by"),
        P("bx", "by"),
        P("bx", "by"),
        P(),
    )
    out_specs = (P(None, "bx", "by", None), P(("bx", "by")))
    return jax.shard_map(local, mesh=mesh, in_specs=in_specs, out_specs=out_specs, check_vma=False)
```

```python
import functools

import jax
import jax.numpy as jnp
from jax import lax
from jax.experimental import pallas as pl
from jax.experimental.pallas import tpu as pltpu
from jax.sharding import PartitionSpec as P

P_DEV = 4
EPS = 0.1
FIELDS = 6
MESH = pl.DeviceIdType.MESH


def smooth_kernel(
    nx, ny, rows_i, rows_j,
    adj_hbm, obj_hbm, rad_hbm, step_hbm, patch_hbm, area_hbm, jac_hbm, orient_hbm, count_hbm, weight_hbm,
    out_ref, force_ref,
    patch_ref, area_ref, jac_ref, orient_ref, count_ref, weight_ref,
    adj, one, obj, rad, step, wall, pack1, pack2, halo1, halo2, turned, mine1, mine2, got1, got2,
    shift, rim2, wpack, whalo, wsend, wrecv,
    load_sem, hsend1, hrecv1, hsend2, hrecv2, psend1, precv1, psend2, precv2,
):
    cells = rows_i * rows_j
    pad = 2 * rows_j
    lanes = adj.shape[2]
    at_x = lax.axis_index("bx")
    at_y = lax.axis_index("by")
    patch_total = P_DEV * nx * ny
    groups = -(-patch_total // lanes)

    small = [
        pltpu.make_async_copy(src, dst, load_sem.at[4 + n])
        for n, (src, dst) in enumerate((
            (weight_hbm, weight_ref), (count_hbm, count_ref), (patch_hbm, patch_ref), (area_hbm, area_ref),
            (jac_hbm, jac_ref), (orient_hbm, orient_ref),
        ))
    ]
    loads = [
        pltpu.make_async_copy(adj_hbm, adj.at[:, pl.ds(pad, cells), :], load_sem.at[0]),
        pltpu.make_async_copy(obj_hbm, obj, load_sem.at[1]),
        pltpu.make_async_copy(rad_hbm, rad, load_sem.at[2]),
        pltpu.make_async_copy(step_hbm, step, load_sem.at[3]),
    ]
    loads[0].start()
    for copy in small:
        copy.start()
    for copy in loads[1:]:
        copy.start()

    barrier = pltpu.get_barrier_semaphore()
    for o in range(1, nx):
        pl.semaphore_signal(barrier, inc=1, device_id=(lax.rem(at_x + o, nx), at_y), device_id_type=MESH)
    for o in range(1, ny):
        pl.semaphore_signal(barrier, inc=1, device_id=(at_x, lax.rem(at_y + o, ny)), device_id_type=MESH)

    zero = jnp.zeros((pad, lanes), jnp.float32)
    for ref in (adj, one):
        for f in range(FIELDS):
            ref[f, pl.ds(0, pad), :] = zero
            ref[f, pl.ds(pad + cells, pad), :] = zero
    pl.semaphore_wait(barrier, nx + ny - 2)

    has = [at_x > 0, at_x < nx - 1, at_y > 0, at_y < ny - 1]
    source_has = [has[1], has[0], has[3], has[2]]
    targets = [
        (lax.min(at_x + 1, nx - 1), at_y),
        (lax.max(at_x - 1, 0), at_y),
        (at_x, lax.min(at_y + 1, ny - 1)),
        (at_x, lax.max(at_y - 1, 0)),
    ]

    def halo_copies(low_rows, high_rows, pack, halo, send_sem, recv_sem):
        sources = [high_rows, low_rows, pack.at[1], pack.at[0]]
        return [
            pltpu.make_async_remote_copy(
                src_ref=sources[s], dst_ref=halo.at[s], send_sem=send_sem.at[s], recv_sem=recv_sem.at[s],
                device_id=targets[s], device_id_type=MESH,
            )
            for s in range(4)
        ]

    def start(copies, s):
        @pl.when(source_has[s])
        def _():
            copies[s].start()

    def pack_faces(ref, pack):
        for side, first in ((0, 0), (1, rows_j - 2)):
            for f in range(FIELDS):
                for layer in range(2):
                    pack[side, f, pl.ds(layer * rows_i, rows_i), :] = ref[
                        f, pl.ds(pad + first + layer, rows_i, stride=rows_j), :
                    ]

    first_copies = halo_copies(
        adj_hbm.at[:, pl.ds(0, pad), :], adj_hbm.at[:, pl.ds(cells - pad, pad), :], pack1, halo1, hsend1, hrecv1
    )
    start(first_copies, 0)
    start(first_copies, 1)
    loads[0].wait()
    pack_faces(adj, pack1)
    start(first_copies, 2)
    start(first_copies, 3)

    for copy in small:
        copy.wait()
    weights = [weight_ref[f] for f in range(FIELDS)]
    patch_t = jnp.transpose(patch_ref[...])
    area_t = jnp.transpose(area_ref[...])
    spot = lax.broadcasted_iota(jnp.int32, (rows_j, rows_i), 1) * rows_j + lax.broadcasted_iota(
        jnp.int32, (rows_j, rows_i), 0
    )
    area_t = jnp.where(spot < count_ref[0, 0], area_t, 0.0)
    lane = lax.broadcasted_iota(jnp.int32, (rows_j, lanes), 1)
    second = lax.broadcasted_iota(jnp.int32, (rows_j, lanes), 0)
    sums = [jnp.zeros((rows_j, lanes), jnp.float32) for _ in range(groups)]
    areas = [jnp.zeros((rows_j, lanes), jnp.float32) for _ in range(groups)]
    for i in range(rows_i):
        weighted = weights[0] * adj[0, pl.ds(pad + i * rows_j, rows_j), :]
        for f in range(1, FIELDS):
            weighted = weighted + weights[f] * adj[f, pl.ds(pad + i * rows_j, rows_j), :]
        area = area_t[:, i : i + 1]
        value = area * weighted[:, 0:1]
        patch = patch_t[:, i : i + 1]
        for r in range(groups):
            hit = patch == lane + r * lanes
            sums[r] = sums[r] + jnp.where(hit, value, 0.0)
            areas[r] = areas[r] + jnp.where(hit, area, 0.0)
    for r in range(groups):
        mine1[pl.ds(r, 1), :] = jnp.sum(sums[r], axis=0, keepdims=True)
        mine1[pl.ds(groups + r, 1), :] = jnp.sum(areas[r], axis=0, keepdims=True)

    x_copies = [
        pltpu.make_async_remote_copy(
            src_ref=mine1, dst_ref=got1.at[o - 1], send_sem=psend1.at[o - 1], recv_sem=precv1.at[o - 1],
            device_id=(lax.rem(at_x + o, nx), at_y), device_id_type=MESH,
        )
        for o in range(1, nx)
    ]
    y_copies = [
        pltpu.make_async_remote_copy(
            src_ref=mine2, dst_ref=got2.at[o - 1], send_sem=psend2.at[o - 1], recv_sem=precv2.at[o - 1],
            device_id=(at_x, lax.rem(at_y + o, ny)), device_id_type=MESH,
        )
        for o in range(1, ny)
    ]
    for copy in x_copies:
        copy.start()

    scale = 0.5 / EPS

    def coupled(direction, g, fields):
        total = (jac_ref[direction, 0, g] * scale) * fields[0]
        for f in range(1, FIELDS):
            total = total + (jac_ref[direction, f, g] * scale) * fields[f]
        return total

    def section(ref, target, offset, factor, with_wall, first_i, last_i):
        def body(i, carry):
            base = pl.multiple_of(i * rows_j, rows_j)

            def rows(f, shift):
                return ref[f, pl.ds(base + (pad + shift), rows_j), :]

            center = [rows(f, 0) for f in range(FIELDS)]
            six = [6.0 * c for c in center]
            total = [None] * FIELDS
            for direction in range(3):
                near, far = [], []
                for f in range(FIELDS):
                    if direction == 0:
                        f1, b1, f2, b2 = (rows(f, s * rows_j) for s in (1, -1, 2, -2))
                    elif direction == 1:
                        f1 = jnp.where(second < rows_j - 1, rows(f, 1), 0.0)
                        b1 = jnp.where(second >= 1, rows(f, -1), 0.0)
                        f2 = jnp.where(second < rows_j - 2, rows(f, 2), 0.0)
                        b2 = jnp.where(second >= 2, rows(f, -2), 0.0)
                    else:
                        c = center[f]
                        f1 = jnp.where(lane < lanes - 1, pltpu.roll(c, lanes - 1, 1), 0.0)
                        b1 = jnp.where(lane >= 1, pltpu.roll(c, 1, 1), 0.0)
                        f2 = jnp.where(lane < lanes - 2, pltpu.roll(c, lanes - 2, 1), 0.0)
                        b2 = jnp.where(lane >= 2, pltpu.roll(c, 2, 1), 0.0)
                    both = f1 + b1
                    near.append(both if direction == 2 else f1 - b1)
                    far.append((f2 + b2) - 4.0 * both + six[f])
                radius = EPS * rad[direction, pl.ds(base, rows_j), :]
                for g in range(FIELDS):
                    term = radius * (far[g] + coupled(direction, g, near))
                    total[g] = term if direction == 0 else total[g] + term
            size = step[pl.ds(base, rows_j), :]
            if factor != 1.0:
                size = factor * size
            at_wall = wall[pl.ds(base, rows_j), :] if with_wall else None
            for g in range(FIELDS):
                whole = total[g] + obj[g, pl.ds(base, rows_j), :]
                if with_wall:
                    whole = whole + weights[g] * at_wall
                start_value = center[g] if ref is adj else adj[g, pl.ds(base + pad, rows_j), :]
                target[g, pl.ds(base + offset, rows_j), :] = start_value - size * whole
            return carry

        lax.fori_loop(first_i, last_i, body, 0)

    def turn(halo, side, flag):
        row = lax.broadcasted_iota(jnp.int32, (lanes, lanes), 0)
        col = lax.broadcasted_iota(jnp.int32, (lanes, lanes), 1)
        goal = jnp.where(flag == 1, lanes - 1 - col, col)
        matrix = jnp.where(row == goal, 1.0, 0.0).astype(jnp.float32)
        values = halo[side].reshape(FIELDS * pad, lanes)
        moved = jnp.dot(values, matrix, precision=lax.Precision.HIGHEST, preferred_element_type=jnp.float32)
        turned[...] = moved.reshape(FIELDS, pad, lanes)

    def correct(halo, side, target, offset, factor):
        direction, high = side // 2, side % 2
        count = rows_j if direction == 0 else rows_i
        layers = rows_i if direction == 0 else rows_j
        near_at, far_at = (0, count) if high else (count, 0)
        edge, inner = (layers - 1, layers - 2) if high else (0, 1)

        def at(layer, extra):
            if direction == 0:
                return pl.ds(extra + layer * rows_j, rows_j)
            return pl.ds(extra + layer, rows_i, stride=rows_j)

        def load(f, first):
            if direction == 0:
                return turned[f, pl.ds(first, count), :]
            return halo[side, f, pl.ds(first, count), :]

        near = [load(f, near_at) for f in range(FIELDS)]
        size_edge = (factor * EPS) * step[at(edge, 0), :] * rad[direction, at(edge, 0), :]
        size_inner = (factor * EPS) * step[at(inner, 0), :] * rad[direction, at(inner, 0), :]
        for g in range(FIELDS):
            mixed = coupled(direction, g, near)
            if not high:
                mixed = -mixed
            change = mixed + (load(g, far_at) - 4.0 * near[g])
            target[g, at(edge, offset), :] = target[g, at(edge, offset), :] - size_edge * change
            target[g, at(inner, offset), :] = target[g, at(inner, offset), :] - size_inner * near[g]

    def finish_halo(copies, halo, target, offset, factor, wall_copies=None):
        for s in range(4):
            @pl.when(has[s])
            def _(s=s):
                copies[s].wait_recv()
                if wall_copies is not None:
                    wall_copies[s].wait_recv()
                    for f in range(FIELDS):
                        halo[s, f] = halo[s, f] - weights[f] * whalo[s]
                if s < 2:
                    turn(halo, s, orient_ref[0, s])
                correct(halo, s, target, offset, factor)

    for copy in loads[1:]:
        copy.wait()
    half = rows_i // 2
    section(adj, one, pad, 0.5, False, 0, half)
    for copy in x_copies:
        copy.wait_recv()
    mine2[...] = functools.reduce(lambda a, b: a + b, [got1[o] for o in range(nx - 1)], mine1[...])
    for copy in y_copies:
        copy.start()
    section(adj, one, pad, 0.5, False, half, rows_i)
    finish_halo(first_copies, halo1, one, pad, 0.5)
    for f in range(FIELDS):
        rim2[0, f] = one[f, pl.ds(pad, pad), :]
        rim2[1, f] = one[f, pl.ds(cells, pad), :]
    second_copies = halo_copies(rim2.at[0], rim2.at[1], pack2, halo2, hsend2, hrecv2)
    start(second_copies, 0)
    start(second_copies, 1)
    pack_faces(one, pack2)
    start(second_copies, 2)
    start(second_copies, 3)
    for copy in y_copies:
        copy.wait_recv()
    summed = functools.reduce(lambda a, b: a + b, [got2[o] for o in range(ny - 1)], mine2[...])
    force = summed[:groups] / (1.0 + summed[groups:])

    for i in range(rows_i):
        patch = patch_t[:, i : i + 1]
        hits = jnp.where(patch == lane, force[0:1], 0.0)
        for r in range(1, groups):
            hits = hits + jnp.where(patch == lane + r * lanes, force[r : r + 1], 0.0)
        face = area_t[:, i : i + 1] * jnp.sum(hits, axis=1, keepdims=True)
        face = jnp.where(lane == 0, face, 0.0)
        wall[pl.ds(i * rows_j, rows_j), :] = face
        moved = 0.5 * step[pl.ds(i * rows_j, rows_j), :] * face
        shift[pl.ds(i * rows_j, rows_j), :] = moved
        for f in range(FIELDS):
            at = pl.ds(pad + i * rows_j, rows_j)
            one[f, at, :] = one[f, at, :] - weights[f] * moved

    for side, first in ((0, 0), (1, rows_j - 2)):
        for layer in range(2):
            wpack[side, pl.ds(layer * rows_i, rows_i), :] = shift[pl.ds(first + layer, rows_i, stride=rows_j), :]
    wall_sources = [shift.at[pl.ds(cells - pad, pad), :], shift.at[pl.ds(0, pad), :], wpack.at[1], wpack.at[0]]
    wall_copies = [
        pltpu.make_async_remote_copy(
            src_ref=wall_sources[s], dst_ref=whalo.at[s], send_sem=wsend.at[s], recv_sem=wrecv.at[s],
            device_id=targets[s], device_id_type=MESH,
        )
        for s in range(4)
    ]
    for s in range(4):
        start(wall_copies, s)

    own = (at_x * ny + at_y) * P_DEV
    place = lax.broadcasted_iota(jnp.int32, (groups, lanes), 0) * lanes + lax.broadcasted_iota(
        jnp.int32, (groups, lanes), 1
    )
    for q in range(P_DEV):
        force_ref[q] = jnp.sum(jnp.where(place == own + q, force, 0.0))

    section(one, out_ref, 0, 1.0, True, 0, rows_i)
    finish_halo(second_copies, halo2, out_ref, 0, 1.0, wall_copies)

    for copies in (first_copies, second_copies, wall_copies):
        for s in range(4):
            @pl.when(source_has[s])
            def _(s=s, copies=copies):
                copies[s].wait_send()
    for copy in x_copies + y_copies:
        copy.wait_send()


def local(
    adjoint_start,
    objective_grad,
    spectral_radius,
    local_step,
    flux_jacobian,
    face_orient,
    wall_count,
    face_patch,
    face_area,
    force_weight,
):
    fields, rows_i, rows_j, lanes = adjoint_start.shape
    cells, pad = rows_i * rows_j, 2 * rows_j
    nx, ny = lax.axis_size("bx"), lax.axis_size("by")
    groups = -(-P_DEV * nx * ny // lanes)
    f32 = jnp.float32
    vmem = pl.BlockSpec(memory_space=pltpu.VMEM)
    smem = pl.BlockSpec(memory_space=pltpu.SMEM)
    hbm = pl.BlockSpec(memory_space=pltpu.HBM)
    dma = pltpu.SemaphoreType.DMA
    result, force = pl.pallas_call(
        functools.partial(smooth_kernel, nx, ny, rows_i, rows_j),
        out_shape=(
            pltpu.VMEM((fields, cells, lanes), f32),
            jax.ShapeDtypeStruct((P_DEV,), f32),
        ),
        in_specs=[hbm] * 10,
        out_specs=(vmem, smem),
        scratch_shapes=[
            pltpu.VMEM(face_patch.shape, jnp.int32),
            pltpu.VMEM(face_area.shape, f32),
            pltpu.SMEM(flux_jacobian.shape, f32),
            pltpu.SMEM(face_orient.shape, jnp.int32),
            pltpu.SMEM(wall_count.shape, jnp.int32),
            pltpu.SMEM(force_weight.shape, f32),
            pltpu.VMEM((fields, cells + 2 * pad, lanes), f32),
            pltpu.VMEM((fields, cells + 2 * pad, lanes), f32),
            pltpu.VMEM((fields, cells, lanes), f32),
            pltpu.VMEM((3, cells, lanes), f32),
            pltpu.VMEM((cells, lanes), f32),
            pltpu.VMEM((cells, lanes), f32),
            pltpu.VMEM((2, fields, 2 * rows_i, lanes), f32),
            pltpu.VMEM((2, fields, 2 * rows_i, lanes), f32),
            pltpu.VMEM((4, fields, pad, lanes), f32),
            pltpu.VMEM((4, fields, pad, lanes), f32),
            pltpu.VMEM((fields, pad, lanes), f32),
            pltpu.VMEM((2 * groups, lanes), f32),
            pltpu.VMEM((2 * groups, lanes), f32),
            pltpu.VMEM((nx - 1, 2 * groups, lanes), f32),
            pltpu.VMEM((ny - 1, 2 * groups, lanes), f32),
            pltpu.VMEM((cells, lanes), f32),
            pltpu.VMEM((2, fields, pad, lanes), f32),
            pltpu.VMEM((2, 2 * rows_i, lanes), f32),
            pltpu.VMEM((4, pad, lanes), f32),
            dma((4,)), dma((4,)),
            dma((10,)), dma((4,)), dma((4,)), dma((4,)), dma((4,)),
            dma((nx - 1,)), dma((nx - 1,)), dma((ny - 1,)), dma((ny - 1,)),
        ],
        compiler_params=pltpu.CompilerParams(
            collective_id=0, has_side_effects=True, vmem_limit_bytes=62 * 1024 * 1024
        ),
    )(
        adjoint_start.reshape(fields, cells, lanes),
        objective_grad.reshape(fields, cells, lanes),
        spectral_radius.reshape(3, cells, lanes),
        local_step.reshape(cells, lanes),
        face_patch,
        face_area,
        flux_jacobian,
        face_orient,
        wall_count,
        force_weight,
    )
    return result.reshape(adjoint_start.shape), force


def solution(mesh):
    in_specs = (
        P(None, "bx", "by", None),
        P(None, "bx", "by", None),
        P(None, "bx", "by", None),
        P("bx", "by", None),
        P(),
        P("bx", None),
        P("bx", "by"),
        P("bx", "by"),
        P("bx", "by"),
        P(),
    )
    out_specs = (P(None, "bx", "by", None), P(("bx", "by")))
    return jax.shard_map(local, mesh=mesh, in_specs=in_specs, out_specs=out_specs, check_vma=False)
```
